32 devices in a mesh: bank: 16 (over z, y, x), tm: 2 (over core).
Axes of the slice: x: 2, y: 2, z: 4, core: 2. Of those that a mesh axis runs over, the one named last changes fastest.
Arguments:
- raw_strain: float32 [3, 2, 2048], P(None, 'tm', 'bank'), may hold values from -6 to 6
- psd_scale: float32 [3, 2, 16], P(None, 'tm', 'bank'), may hold values from 0.25 to 8
- basis_filters: bfloat16 [16, 128, 128], P('bank'), may hold values from -0.5 to 0.5
- recon_matrix: bfloat16 [16, 128, 2, 768], P('bank', None, None, 'tm'), may hold values from -0.5 to 0.5
- bin_taps: int32 [16], P('bank'), may hold values from 32 to 128, as said below
- bin_band: int32 [16], P('bank'), may hold values from 0 to 2, as said below
- bin_window: int32 [16], P('bank'), may hold values from 0 to 7
- window_start: int32 [8], replicated, may hold values from 512 to 1536, as said below
Outputs:
- peak_snr: float32 [3, 12288], P(None, ('bank', 'tm'))
- mean_power: float32 [3, 12288], P(None, ('bank', 'tm'))
- loudest: float32 [3, 4096], P(None, 'tm')
The draws below stay inside these ranges and needn't reach their ends.
Inputs may be any that keep to these rules, and one draw needn't show every extreme that they name: `bin_taps`: some bin uses 128 taps and some the fewest. `bin_band`: the lowest and the highest band each occur. `window_start`: a window starts at each end of the range.
All inputs are finite; a program needn't handle non-finite values.
Results may differ from the reference program's by a relative error of at most 0.0035.
Values may be sent and summed in bfloat16 or wider, within the bound.
A program may use at most 64 MiB of HBM per device.

```python
import math
import jax
import jax.numpy as jnp
from jax import lax

DET = 3
PERIOD_READINGS = 2048
TAPS = 128
NB = 128
TPL_BIN = 768
NWIN = 8
PAST_REACH_LOW = 512
SEGS = 2
BINS = 16
PIECE = 128
N_TM = 2


def draw_psd_scale(key, part):
    key = jax.random.fold_in(key, 11)
    position = (jnp.arange(SEGS)[:, None] * BINS + jnp.arange(BINS)[None, :]).astype(jnp.float32) / max(SEGS * BINS - 1, 1)
    rising = jnp.exp(math.log(3.0) * position)
    roughness = jnp.exp(jax.random.uniform(key, (DET, SEGS, BINS), jnp.float32, math.log(0.5), math.log(2.0)))
    return (rising[None, :, :] * roughness).astype(jnp.float32)


def draw_bin_taps(key, part):
    key = jax.random.fold_in(key, 12)
    key_vals, key_perm = jax.random.split(key)
    values = jax.random.randint(key_vals, (BINS,), TAPS // 4, TAPS + 1, dtype=jnp.int32)
    chosen = jax.random.permutation(key_perm, BINS)
    values = values.at[chosen[0]].set(TAPS)
    return values.at[chosen[1]].set(TAPS // 4)


def draw_bin_band(key, part):
    key = jax.random.fold_in(key, 13)
    key_vals, key_perm = jax.random.split(key)
    values = jax.random.randint(key_vals, (BINS,), 0, 3, dtype=jnp.int32)
    chosen = jax.random.permutation(key_perm, BINS)
    values = values.at[chosen[0]].set(0)
    return values.at[chosen[1]].set(2)


def draw_window_start(key, part):
    key = jax.random.fold_in(key, 14)
    key_vals, key_perm = jax.random.split(key)
    values = jax.random.randint(key_vals, (NWIN,), PAST_REACH_LOW, PERIOD_READINGS - PAST_REACH_LOW + 1, dtype=jnp.int32)
    chosen = jax.random.permutation(key_perm, NWIN)
    values = values.at[chosen[0]].set(PAST_REACH_LOW)
    return values.at[chosen[1]].set(PERIOD_READINGS - PAST_REACH_LOW)


def place_ends(values, own_key, smallest, largest):
    spot = [jax.random.randint(jax.random.fold_in(own_key, axis), (), 0, length) for axis, length in enumerate(values.shape)]
    longest = values.shape.index(max(values.shape))
    neighbour = spot[:longest] + [(spot[longest] + 1) % values.shape[longest]] + spot[longest + 1:]
    return values.at[tuple(spot)].set(smallest).at[tuple(neighbour)].set(largest)


def steps_of(own_key, dims, cuts, low, largest):
    def one(axis_at, parts):
        draws = jax.random.uniform(jax.random.fold_in(jax.random.fold_in(own_key, 6), axis_at), (parts,), jnp.float32, low / len(cuts), largest / len(cuts))
        return jnp.repeat(jnp.exp(draws), dims[axis_at] // parts).reshape((-1,) + (1,) * (len(dims) - axis_at - 1))

    loudness = one(*cuts[0])
    for cut in cuts[1:]:
        loudness = loudness * one(*cut)
    return loudness


def gaussian(stream_key, dims, spread, limit, shards=(), kind=jnp.bfloat16):
    values = jax.random.normal(stream_key, dims, jnp.float32) * spread
    if len(shards) > 0:
        values = steps_of(stream_key, dims, shards, -0.22, 0.18) * values
    return jnp.clip(values, min=-limit, max=limit).astype(kind)


def setup_inputs(seed: int = 0) -> dict:
    arg_keys = jax.random.split(jax.random.key(seed), 9)
    return {
        "raw_strain": gaussian(arg_keys[0], (DET, SEGS, PERIOD_READINGS), 1.0, 6.0, ((1, 2), (2, 16)), jnp.float32),
        "psd_scale": draw_psd_scale(jax.random.fold_in(arg_keys[8], 71), 0),
        "basis_filters": gaussian(arg_keys[2], (BINS, TAPS, NB), TAPS ** -0.5, 0.5, ((0, 16),)),
        "recon_matrix": gaussian(arg_keys[3], (BINS, NB, 2, TPL_BIN), NB ** -0.5, 0.5, ((0, 16), (3, 2))),
        "bin_taps": draw_bin_taps(jax.random.fold_in(arg_keys[8], 71), 0),
        "bin_band": draw_bin_band(jax.random.fold_in(arg_keys[8], 71), 0),
        "bin_window": place_ends(jax.random.randint(arg_keys[6], (BINS,), 0, NWIN), jax.random.fold_in(arg_keys[6], 1), 0, NWIN - 1).astype(jnp.int32),
        "window_start": draw_window_start(jax.random.fold_in(arg_keys[8], 71), 0),
    }


epsilon = 1e-06

def averaged_series(lengthened_series, decimation_ratio):
    zero_extended = jnp.concatenate([jnp.zeros((lengthened_series.shape[0], 3), jnp.float32), lengthened_series.astype(jnp.float32)], axis=1)
    extent_total = lengthened_series.shape[1]
    accumulated_total = jnp.zeros((lengthened_series.shape[0], extent_total), jnp.float32)
    for delayed_series in range(4):
        accumulated_total = accumulated_total + jnp.where(delayed_series < decimation_ratio, zero_extended[:, 3 - delayed_series:3 - delayed_series + extent_total], jnp.float32(0.0))
    return (accumulated_total / decimation_ratio.astype(jnp.float32)).astype(jnp.bfloat16)

def reference(raw_strain, psd_scale, basis_filters, recon_matrix, bin_taps, bin_band, bin_window, window_start):
    detector_readings = PERIOD_READINGS * N_TM
    scaled = (raw_strain * jnp.repeat(psd_scale, PIECE, axis=2)).reshape(DET, detector_readings)
    norm_scale = jnp.sqrt(lax.optimization_barrier(jnp.mean(scaled * scaled, axis=1)) + epsilon)
    whitened = (scaled / norm_scale[:, None]).astype(jnp.bfloat16)
    lengthened_series = jnp.concatenate([jnp.zeros((DET, PAST_REACH_LOW), jnp.bfloat16), whitened], axis=1)
    result_moments = jnp.arange(detector_readings, dtype=jnp.int32)
    kernel_coefficient_slot = jnp.arange(TAPS, dtype=jnp.int32)

    def per_bin(carried, bin_id):
        frequency_level = bin_band[bin_id]
        decimation_ratio = jnp.where(frequency_level == 0, 1, jnp.where(frequency_level == 1, 2, 4)).astype(jnp.int32)
        gentle_average = averaged_series(lengthened_series, decimation_ratio)
        masked_basis = basis_filters[bin_id] * (kernel_coefficient_slot < bin_taps[bin_id]).astype(jnp.bfloat16)[:, None]
        reading_locations = (PAST_REACH_LOW + result_moments[:, None] - decimation_ratio * kernel_coefficient_slot[None, :]).astype(jnp.int32)
        windows = gentle_average[:, reading_locations].astype(jnp.float32)
        filtered = jnp.einsum('dtk,kn->dtn', windows, masked_basis.astype(jnp.float32)).astype(jnp.bfloat16)
        recon_mat = recon_matrix[bin_id].reshape(NB, 2 * TPL_BIN).astype(jnp.float32)
        complex_snr = jnp.einsum('dtn,nm->dtm', filtered.astype(jnp.float32), recon_mat)
        powers = complex_snr[:, :, :TPL_BIN] ** 2 + complex_snr[:, :, TPL_BIN:] ** 2
        interval_opening_reading = window_start[bin_window[bin_id]]
        inside_limits = (result_moments >= interval_opening_reading) & (result_moments < interval_opening_reading + PERIOD_READINGS)
        masked = jnp.where(inside_limits[None, :, None], powers, jnp.float32(0.0))
        peak_bin = lax.optimization_barrier(jnp.max(masked, axis=1))
        mean_bin = lax.optimization_barrier(jnp.sum(masked, axis=1)) / PERIOD_READINGS
        series = lax.optimization_barrier(jnp.max(masked, axis=2))
        return (jnp.maximum(carried, series), (peak_bin, mean_bin))
    loudest, (peaks, means) = lax.scan(per_bin, jnp.zeros((DET, detector_readings), jnp.float32), jnp.arange(BINS, dtype=jnp.int32))
    peak_snr = jnp.transpose(peaks, (1, 0, 2)).reshape(DET, BINS * TPL_BIN)
    mean_power = jnp.transpose(means, (1, 0, 2)).reshape(DET, BINS * TPL_BIN)
    return (peak_snr, mean_power, loudest)
```

```python
import functools

import jax
import jax.numpy as jnp
from jax import lax
from jax.experimental import pallas as pl
from jax.experimental.pallas import tpu as pltpu
from jax.sharding import PartitionSpec as P

EPSILON = 1e-06
LANES = 128
SEG_CHUNKS = 16
CHUNKS = 32
WIN = 2048
FIRST = 4
LAST = 28
STEPS = 9
REL = 2 * STEPS
PAD = 8
DET = 3
SLOT = 4
MESH = pl.DeviceIdType.MESH


def wait_bytes(ref, sem):
    pltpu.make_async_copy(ref, ref, sem).wait()


def fold_filters(basis_ref, recon_ref, taps, gains):
    features = basis_ref.shape[2]
    tap = lax.broadcasted_iota(jnp.int32, basis_ref.shape[1:], 0)
    basis = jnp.where(tap < taps, basis_ref[0].astype(jnp.float32), 0.0).astype(jnp.bfloat16)
    row = lax.broadcasted_iota(jnp.int32, (features, 2 * features), 0)
    col = lax.broadcasted_iota(jnp.int32, (features, 2 * features), 1)
    pairs = recon_ref[0].reshape(2 * features, recon_ref.shape[3])
    for c in range(2):
        spread = jnp.where(col == 2 * row + c, 1.0, 0.0).astype(jnp.bfloat16)
        wide = jnp.dot(basis, spread, preferred_element_type=jnp.float32).astype(jnp.bfloat16)
        g = jnp.dot(wide, pairs, preferred_element_type=jnp.float32)
        gt = g.T.astype(jnp.bfloat16)
        gains[:, 8 * c : 8 * c + 8, :] = gt.reshape(-1, 8, gt.shape[1])


def whiten_and_smooth(strain, d, rate, smooth):
    x = strain[:, d, :]
    ss = jnp.sum(jnp.sum(x * x, axis=0, keepdims=True), axis=1, keepdims=True)
    norm = jnp.sqrt(ss / (CHUNKS * LANES) + EPSILON)
    w = (x / norm).astype(jnp.bfloat16).astype(jnp.float32)
    lane = lax.broadcasted_iota(jnp.int32, w.shape, 1)
    row = lax.broadcasted_iota(jnp.int32, w.shape, 0)
    before = jnp.where(row == 0, 0.0, pltpu.roll(w, 1, 0))
    total = w
    for j in range(1, 4):
        late = jnp.where(lane < j, pltpu.roll(before, j, 1), pltpu.roll(w, j, 1))
        total = total + jnp.where(j < rate, late, 0.0)
    mean = total / rate.astype(jnp.float32)
    smooth[d] = mean.astype(jnp.bfloat16).astype(jnp.float32)


def lay_delays(d, rate, start, smooth, octet):
    count = REL + 4
    y = jnp.broadcast_to(smooth[d, pl.ds(start - 4, count), :][:, None, :], (count, 8, LANES))
    lane = lax.broadcasted_iota(jnp.int32, y.shape, 2)
    sub = lax.broadcasted_iota(jnp.int32, y.shape, 1)
    for bit in (1, 2, 4):
        shift = rate * bit
        r = pltpu.roll(y, shift, 2)
        late = jnp.where(lane < shift, jnp.concatenate([r[:1], r[:-1]], axis=0), r)
        y = jnp.where((sub & bit) != 0, late, y)
    octet[d] = y


def lay_taps(h, d, rate, offset, octet, taps_ref):
    lane = lax.broadcasted_iota(jnp.int32, (REL, 8, LANES), 2)
    when = lax.broadcasted_iota(jnp.int32, (REL, 8, LANES), 0) * LANES + lane
    inside = (when >= offset) & (when < offset + WIN)
    halves = []
    for e in range(2):
        eights = rate * (2 * h + e)
        back = eights // 16
        shift = 8 * (eights - 16 * back)
        r = pltpu.roll(octet[d, pl.ds(3 - back, REL + 1)], shift, 2)
        halves.append(jnp.where(inside, jnp.where(lane < shift, r[:-1], r[1:]), 0.0))
    both = jnp.concatenate(halves, axis=1).astype(jnp.bfloat16)
    at = pl.ds(pl.multiple_of(16 * h, 16), 16)
    for i in range(REL):
        taps_ref[d, at, LANES * i : LANES * (i + 1)] = both[i]


def score_pair(p, taps_ref, gains, peak, total, series):
    weights = gains[...]
    weights = weights.reshape(-1, weights.shape[2])
    for d in range(DET):
        at = pl.ds(pl.multiple_of(2 * LANES * p, 2 * LANES), 2 * LANES)
        snr = jnp.dot(weights, taps_ref[d, :, at], preferred_element_type=jnp.float32)
        snr = snr.reshape(-1, 2, 8, 2 * LANES)
        re, im = snr[:, 0], snr[:, 1]
        power = re * re + im * im
        left, right = power[:, :, :LANES], power[:, :, LANES:]
        peak[d] = jnp.maximum(peak[d], jnp.maximum(left, right))
        total[d] = total[d] + (left + right)
        loud = jnp.max(jnp.max(power, axis=0), axis=0, keepdims=True)
        series[PAD + 2 * p, d : d + 1, :] = loud[:, :LANES]
        series[PAD + 2 * p + 1, d : d + 1, :] = loud[:, LANES:]


def finish_templates(peak, total, peak_ref, mean_ref):
    for d in range(DET):
        top = peak[d].reshape(-1, LANES).T
        peak_ref[d : d + 1, :] = jnp.max(top, axis=0, keepdims=True)
        add = total[d].reshape(-1, LANES).T
        mean_ref[d : d + 1, :] = jnp.sum(add, axis=0, keepdims=True) * (1.0 / WIN)


def settings(taps_s, band_s, window_s, start_s):
    band = band_s[0]
    rate = jnp.where(band == 0, 1, jnp.where(band == 1, 2, 4)).astype(jnp.int32)
    opening = jnp.clip(start_s[window_s[0]], FIRST * LANES, LAST * LANES - WIN)
    start = opening // LANES
    return taps_s[0], rate, start, opening - LANES * start


def clear(peak, total, series):
    peak[...] = jnp.zeros_like(peak)
    total[...] = jnp.zeros_like(total)
    series[...] = jnp.zeros_like(series)


def lay_all(strain, rate, start, offset, smooth, octet, taps_ref):
    for d in range(DET):
        whiten_and_smooth(strain, d, rate, smooth)
    for d in range(DET):
        lay_delays(d, rate, start, smooth, octet)

    def body(h, carry):
        for d in range(DET):
            lay_taps(h, d, rate, offset, octet, taps_ref)
        return carry

    lax.fori_loop(0, 8, body, 0)


def local_kernel(
    taps_s, band_s, window_s, start_s, strain, basis_ref, recon_ref,
    peak_ref, mean_ref, loud_ref,
    smooth, octet, taps_ref, gains, peak, total, series,
):
    taps, rate, start, offset = settings(taps_s, band_s, window_s, start_s)
    clear(peak, total, series)
    fold_filters(basis_ref, recon_ref, taps, gains)
    lay_all(strain, rate, start, offset, smooth, octet, taps_ref)
    lax.fori_loop(
        0, STEPS, lambda p, c: (score_pair(p, taps_ref, gains, peak, total, series), c)[1], 0
    )
    loud_ref[...] = jnp.zeros_like(loud_ref)
    for q in range(FIRST, LAST):
        loud_ref[q] = series[PAD + q - start]
    finish_templates(peak, total, peak_ref, mean_ref)


def linked_kernel(
    n_bank,
    taps_s, band_s, window_s, start_s, scale_s, raw_ref, basis_ref, recon_ref,
    peak_ref, mean_ref, loud_ref,
    mine, strain, smooth, octet, taps_ref, gains, peak, total, series,
    parts, found, best, heard,
    gather_out, gather_in, part_out, part_in, best_out, best_in,
):
    bank, tm = lax.axis_index("bank"), lax.axis_index("tm")
    me = tm * n_bank + bank
    others = 2 * n_bank - 1

    def place(q):
        return (lax.rem(q, n_bank), q // n_bank)

    barrier = pltpu.get_barrier_semaphore()

    def greet(i, carry):
        to = place(lax.rem(me + i, 2 * n_bank))
        pl.semaphore_signal(barrier, inc=1, device_id=to, device_id_type=MESH)
        return carry

    lax.fori_loop(1, 2 * n_bank, greet, 0)
    taps, rate, start, offset = settings(taps_s, band_s, window_s, start_s)
    for d in range(DET):
        mine[d : d + 1, :] = raw_ref[d] * scale_s[d, 0, 0]
    mine[DET:SLOT, :] = jnp.zeros((SLOT - DET, LANES), jnp.float32)
    strain[me] = mine[...]
    pl.semaphore_wait(barrier, others)

    def share(i, carry):
        to = place(lax.rem(me + i, 2 * n_bank))
        pltpu.make_async_remote_copy(
            src_ref=mine, dst_ref=strain.at[me], send_sem=gather_out, recv_sem=gather_in,
            device_id=to, device_id_type=MESH,
        ).start()
        return carry

    lax.fori_loop(1, 2 * n_bank, share, 0)
    clear(peak, total, series)
    fold_filters(basis_ref, recon_ref, taps, gains)
    wait_bytes(strain.at[pl.ds(0, others)], gather_in)
    lay_all(strain, rate, start, offset, smooth, octet, taps_ref)
    lax.fori_loop(
        0, STEPS, lambda p, c: (score_pair(p, taps_ref, gains, peak, total, series), c)[1], 0
    )
    for q in range(FIRST, LAST):
        parts[q - FIRST] = series[PAD + q - start]

    owner = (me >= FIRST) & (me < LAST)

    def spread(q, carry):
        @pl.when(q != me)
        def _():
            pltpu.make_async_remote_copy(
                src_ref=parts.at[q - FIRST], dst_ref=found.at[me],
                send_sem=part_out, recv_sem=part_in,
                device_id=place(q), device_id_type=MESH,
            ).start()

        return carry

    lax.fori_loop(FIRST, LAST, spread, 0)

    @pl.when(owner)
    def _():
        found[me] = parts[me - FIRST]
        wait_bytes(found.at[pl.ds(0, others)], part_in)
        best[...] = jnp.max(found[...], axis=0)
        heard[bank] = best[...]

        def announce(i, carry):
            to = (lax.rem(bank + i, n_bank), tm)
            pltpu.make_async_remote_copy(
                src_ref=best, dst_ref=heard.at[bank], send_sem=best_out, recv_sem=best_in,
                device_id=to, device_id_type=MESH,
            ).start()
            return carry

        lax.fori_loop(1, n_bank, announce, 0)

    finish_templates(peak, total, peak_ref, mean_ref)
    wait_bytes(strain.at[pl.ds(0, others)], gather_out)

    @pl.when(owner)
    def _():
        wait_bytes(parts.at[pl.ds(0, LAST - FIRST - 1)], part_out)
        wait_bytes(heard.at[pl.ds(0, SEG_CHUNKS - FIRST - 1)], best_in)
        wait_bytes(heard.at[pl.ds(0, n_bank - 1)], best_out)

    @pl.when(jnp.logical_not(owner))
    def _():
        wait_bytes(parts, part_out)
        wait_bytes(heard.at[pl.ds(0, SEG_CHUNKS - FIRST)], best_in)

    for c in range(n_bank):
        low, high = FIRST, LAST - SEG_CHUNKS
        block = heard[c, 0:DET, :]
        if c < low:
            block = jnp.where(tm == 0, 0.0, block)
        if c >= high:
            block = jnp.where(tm == 1, 0.0, block)
        loud_ref[:, LANES * c : LANES * (c + 1)] = block


def scratch(taps, templates):
    groups = templates // 8
    return [
        pltpu.VMEM((DET, CHUNKS, LANES), jnp.float32),
        pltpu.VMEM((DET, REL + 4, 8, LANES), jnp.float32),
        pltpu.VMEM((DET, taps, REL * LANES), jnp.bfloat16),
        pltpu.VMEM((groups, 16, taps), jnp.bfloat16),
        pltpu.VMEM((DET, groups, 8, LANES), jnp.float32),
        pltpu.VMEM((DET, groups, 8, LANES), jnp.float32),
        pltpu.VMEM((CHUNKS, SLOT, LANES), jnp.float32),
    ]


VMEM = pl.BlockSpec(memory_space=pltpu.VMEM)
SMEM = pl.BlockSpec(memory_space=pltpu.SMEM)
VMEM_LIMIT = 32 * 1024 * 1024


def per_device(
    raw_strain, psd_scale, basis_filters, recon_matrix, bin_taps, bin_band, bin_window, window_start
):
    n_bank, n_tm = lax.axis_size("bank"), lax.axis_size("tm")
    taps, templates = basis_filters.shape[1], recon_matrix.shape[3]
    stats = jax.ShapeDtypeStruct((DET, templates), jnp.float32)
    scalars = (bin_taps, bin_band, bin_window, window_start)
    if raw_strain.shape[2] == LANES and n_bank == SEG_CHUNKS and n_tm == 2:
        slots = pltpu.VMEM((CHUNKS, SLOT, LANES), jnp.float32)
        return pl.pallas_call(
            functools.partial(linked_kernel, n_bank),
            out_shape=(stats, stats, jax.ShapeDtypeStruct((DET, n_bank * LANES), jnp.float32)),
            in_specs=[SMEM] * 5 + [VMEM] * 3,
            out_specs=(VMEM,) * 3,
            scratch_shapes=[pltpu.VMEM((SLOT, LANES), jnp.float32), slots]
            + scratch(taps, templates)
            + [
                pltpu.VMEM((LAST - FIRST, SLOT, LANES), jnp.float32),
                slots,
                pltpu.VMEM((SLOT, LANES), jnp.float32),
                pltpu.VMEM((n_bank, SLOT, LANES), jnp.float32),
            ]
            + [pltpu.SemaphoreType.DMA] * 6,
            compiler_params=pltpu.CompilerParams(
                collective_id=0, has_side_effects=True, vmem_limit_bytes=VMEM_LIMIT
            ),
        )(*scalars, psd_scale, raw_strain, basis_filters, recon_matrix)

    scaled = raw_strain * psd_scale
    whole = lax.all_gather(scaled, "bank", axis=2, tiled=True)
    whole = lax.all_gather(whole, "tm", axis=1, tiled=True)
    blocks = whole.reshape(DET, CHUNKS, LANES).transpose(1, 0, 2)
    blocks = jnp.pad(blocks, ((0, 0), (0, SLOT - DET), (0, 0)))
    peak, mean, loud = pl.pallas_call(
        local_kernel,
        out_shape=(stats, stats, jax.ShapeDtypeStruct((CHUNKS, SLOT, LANES), jnp.float32)),
        in_specs=[SMEM] * 4 + [VMEM] * 3,
        out_specs=(VMEM,) * 3,
        scratch_shapes=scratch(taps, templates),
        compiler_params=pltpu.CompilerParams(vmem_limit_bytes=VMEM_LIMIT),
    )(*scalars, blocks, basis_filters, recon_matrix)
    loud = lax.pmax(loud[:, :DET].transpose(1, 0, 2).reshape(DET, CHUNKS * LANES), ("bank", "tm"))
    length = CHUNKS * LANES // n_tm
    return peak, mean, lax.dynamic_slice_in_dim(loud, lax.axis_index("tm") * length, length, 1)


def solution(mesh):
    return jax.shard_map(
        per_device,
        mesh=mesh,
        in_specs=(
            P(None, "tm", "bank"),
            P(None, "tm", "bank"),
            P("bank", None, None),
            P("bank", None, None, "tm"),
            P("bank"),
            P("bank"),
            P("bank"),
            P(),
        ),
        out_specs=(P(None, ("bank", "tm")), P(None, ("bank", "tm")), P(None, "tm")),
        check_vma=False,
    )
```

```python
import functools

import jax
import jax.numpy as jnp
from jax import lax
from jax.experimental import pallas as pl
from jax.experimental.pallas import tpu as pltpu
from jax.sharding import PartitionSpec as P

EPSILON = 1e-06
LANES = 128
SEG_CHUNKS = 16
CHUNKS = 32
WIN = 2048
FIRST = 4
LAST = 28
STEPS = 9
REL = 2 * STEPS
PAD = 8
DET = 3
SLOT = 4
LINE, PLANE, GROUP = 4, 4, 8
SHARE = (LAST - FIRST) // GROUP
MESH = pl.DeviceIdType.MESH


def wait_bytes(ref, sem):
    pltpu.make_async_copy(ref, ref, sem).wait()


def fold_filters(basis_ref, recon_ref, taps, gains):
    features = basis_ref.shape[2]
    tap = lax.broadcasted_iota(jnp.int32, basis_ref.shape[1:], 0)
    basis = jnp.where(tap < taps, basis_ref[0].astype(jnp.float32), 0.0).astype(jnp.bfloat16)
    row = lax.broadcasted_iota(jnp.int32, (features, 2 * features), 0)
    col = lax.broadcasted_iota(jnp.int32, (features, 2 * features), 1)
    pairs = recon_ref[0].reshape(2 * features, recon_ref.shape[3])
    for c in range(2):
        spread = jnp.where(col == 2 * row + c, 1.0, 0.0).astype(jnp.bfloat16)
        wide = jnp.dot(basis, spread, preferred_element_type=jnp.float32).astype(jnp.bfloat16)
        g = jnp.dot(wide, pairs, preferred_element_type=jnp.float32)
        gt = g.T.astype(jnp.bfloat16)
        gains[:, 8 * c : 8 * c + 8, :] = gt.reshape(-1, 8, gt.shape[1])


def whiten_and_smooth(strain, d, rate, smooth):
    x = strain[:, d, :]
    ss = jnp.sum(jnp.sum(x * x, axis=0, keepdims=True), axis=1, keepdims=True)
    norm = jnp.sqrt(ss / (CHUNKS * LANES) + EPSILON)
    w = (x / norm).astype(jnp.bfloat16).astype(jnp.float32)
    lane = lax.broadcasted_iota(jnp.int32, w.shape, 1)
    row = lax.broadcasted_iota(jnp.int32, w.shape, 0)
    before = jnp.where(row == 0, 0.0, pltpu.roll(w, 1, 0))
    total = w
    for j in range(1, 4):
        late = jnp.where(lane < j, pltpu.roll(before, j, 1), pltpu.roll(w, j, 1))
        total = total + jnp.where(j < rate, late, 0.0)
    mean = total / rate.astype(jnp.float32)
    smooth[d] = mean.astype(jnp.bfloat16).astype(jnp.float32)


def lay_delays(d, rate, start, smooth, octet):
    count = REL + 4
    y = jnp.broadcast_to(smooth[d, pl.ds(start - 4, count), :][:, None, :], (count, 8, LANES))
    lane = lax.broadcasted_iota(jnp.int32, y.shape, 2)
    sub = lax.broadcasted_iota(jnp.int32, y.shape, 1)
    for bit in (1, 2, 4):
        shift = rate * bit
        r = pltpu.roll(y, shift, 2)
        late = jnp.where(lane < shift, jnp.concatenate([r[:1], r[:-1]], axis=0), r)
        y = jnp.where((sub & bit) != 0, late, y)
    octet[d] = y


def lay_taps(h, d, rate, offset, octet, taps_ref):
    lane = lax.broadcasted_iota(jnp.int32, (REL, 8, LANES), 2)
    when = lax.broadcasted_iota(jnp.int32, (REL, 8, LANES), 0) * LANES + lane
    inside = (when >= offset) & (when < offset + WIN)
    halves = []
    for e in range(2):
        eights = rate * (2 * h + e)
        back = eights // 16
        shift = 8 * (eights - 16 * back)
        r = pltpu.roll(octet[d, pl.ds(3 - back, REL + 1)], shift, 2)
        halves.append(jnp.where(inside, jnp.where(lane < shift, r[:-1], r[1:]), 0.0))
    both = jnp.concatenate(halves, axis=1).astype(jnp.bfloat16)
    at = pl.ds(pl.multiple_of(16 * h, 16), 16)
    for i in range(REL):
        taps_ref[d, at, LANES * i : LANES * (i + 1)] = both[i]


def score_pair(p, taps_ref, gains, peak, total, series):
    weights = gains[...]
    weights = weights.reshape(-1, weights.shape[2])
    for d in range(DET):
        at = pl.ds(pl.multiple_of(2 * LANES * p, 2 * LANES), 2 * LANES)
        snr = jnp.dot(weights, taps_ref[d, :, at], preferred_element_type=jnp.float32)
        snr = snr.reshape(-1, 2, 8, 2 * LANES)
        re, im = snr[:, 0], snr[:, 1]
        power = re * re + im * im
        left, right = power[:, :, :LANES], power[:, :, LANES:]
        peak[d] = jnp.maximum(peak[d], jnp.maximum(left, right))
        total[d] = total[d] + (left + right)
        loud = jnp.max(jnp.max(power, axis=0), axis=0, keepdims=True)
        series[PAD + 2 * p, d : d + 1, :] = loud[:, :LANES]
        series[PAD + 2 * p + 1, d : d + 1, :] = loud[:, LANES:]


def finish_templates(peak, total, peak_ref, mean_ref):
    for d in range(DET):
        top = peak[d].reshape(-1, LANES).T
        peak_ref[d : d + 1, :] = jnp.max(top, axis=0, keepdims=True)
        add = total[d].reshape(-1, LANES).T
        mean_ref[d : d + 1, :] = jnp.sum(add, axis=0, keepdims=True) * (1.0 / WIN)


def settings(taps_s, band_s, window_s, start_s):
    band = band_s[0]
    rate = jnp.where(band == 0, 1, jnp.where(band == 1, 2, 4)).astype(jnp.int32)
    opening = jnp.clip(start_s[window_s[0]], FIRST * LANES, LAST * LANES - WIN)
    start = opening // LANES
    return taps_s[0], rate, start, opening - LANES * start


def clear(peak, total, series):
    peak[...] = jnp.zeros_like(peak)
    total[...] = jnp.zeros_like(total)
    series[...] = jnp.zeros_like(series)


def lay_all(strain, rate, start, offset, smooth, octet, taps_ref):
    for d in range(DET):
        whiten_and_smooth(strain, d, rate, smooth)
    for d in range(DET):
        lay_delays(d, rate, start, smooth, octet)

    def body(h, carry):
        for d in range(DET):
            lay_taps(h, d, rate, offset, octet, taps_ref)
        return carry

    lax.fori_loop(0, 8, body, 0)


def local_kernel(
    taps_s, band_s, window_s, start_s, strain, basis_ref, recon_ref,
    peak_ref, mean_ref, loud_ref,
    smooth, octet, taps_ref, gains, peak, total, series,
):
    taps, rate, start, offset = settings(taps_s, band_s, window_s, start_s)
    clear(peak, total, series)
    fold_filters(basis_ref, recon_ref, taps, gains)
    lay_all(strain, rate, start, offset, smooth, octet, taps_ref)
    lax.fori_loop(
        0, STEPS, lambda p, c: (score_pair(p, taps_ref, gains, peak, total, series), c)[1], 0
    )
    loud_ref[...] = jnp.zeros_like(loud_ref)
    for q in range(FIRST, LAST):
        loud_ref[q] = series[PAD + q - start]
    finish_templates(peak, total, peak_ref, mean_ref)


def linked_kernel(
    taps_h, band_h, window_h, start_h, scale_h, raw_h, basis_h, recon_h,
    peak_ref, mean_ref, loud_ref,
    taps_s, band_s, window_s, start_s, scale_s, raw_ref, basis_ref, recon_ref,
    strain, ordered, smooth, octet, taps_ref, gains, peak, total, series,
    parts, found, plane_best, best, heard,
    fetched, lines_out, lines_in, plane_out, plane_in,
    part_out, part_in, line_out, line_in, best_out, best_in,
):
    bank, tm = lax.axis_index("bank"), lax.axis_index("tm")
    z, xy = bank // PLANE, lax.rem(bank, PLANE)
    mine = tm * PLANE + xy

    def along(i):
        return (lax.rem(z + i, LINE) * PLANE + xy, tm)

    def across(g):
        return (z * PLANE + lax.rem(g, PLANE), g // PLANE)

    def send(src, dst, out, into, to):
        pltpu.make_async_remote_copy(
            src_ref=src, dst_ref=dst, send_sem=out, recv_sem=into,
            device_id=to, device_id_type=MESH,
        ).start()

    barrier = pltpu.get_barrier_semaphore()
    for i in range(1, LINE):
        pl.semaphore_signal(barrier, inc=1, device_id=along(i), device_id_type=MESH)
    for i in range(1, GROUP):
        to = across(lax.rem(mine + i, GROUP))
        pl.semaphore_signal(barrier, inc=1, device_id=to, device_id_type=MESH)
    pairs = (
        (scale_h, scale_s), (raw_h, raw_ref), (taps_h, taps_s), (band_h, band_s),
        (window_h, window_s), (start_h, start_s), (basis_h, basis_ref), (recon_h, recon_ref),
    )
    fetches = [pltpu.make_async_copy(a, b, fetched.at[i]) for i, (a, b) in enumerate(pairs)]
    for fetch in fetches:
        fetch.start()
    fetches[0].wait()
    fetches[1].wait()
    block = jnp.concatenate([raw_ref[d] * scale_s[d] for d in range(DET)], axis=0)
    here = mine * LINE + z
    strain[here] = jnp.concatenate([block, jnp.zeros((SLOT - DET, LANES), jnp.float32)], axis=0)
    pl.semaphore_wait(barrier, LINE + GROUP - 2)
    for i in range(1, LINE):
        send(strain.at[here], strain.at[here], lines_out, lines_in, along(i))
    clear(peak, total, series)
    for fetch in fetches[2:]:
        fetch.wait()
    taps, rate, start, offset = settings(taps_s, band_s, window_s, start_s)
    run = strain.at[pl.ds(mine * LINE, LINE)]
    wait_bytes(strain.at[pl.ds(0, LINE - 1)], lines_in)
    for i in range(1, GROUP):
        send(run, run, plane_out, plane_in, across(lax.rem(mine + i, GROUP)))
    fold_filters(basis_ref, recon_ref, taps, gains)
    wait_bytes(strain.at[pl.ds(0, (GROUP - 1) * LINE)], plane_in)
    for q in range(CHUNKS):
        t, line, spot = q // SEG_CHUNKS, q % SEG_CHUNKS // PLANE, q % PLANE
        ordered[q] = strain[(t * PLANE + spot) * LINE + line]
    lay_all(ordered, rate, start, offset, smooth, octet, taps_ref)

    def pass_on(g):
        for i in range(SHARE):
            parts[g, i] = series[PAD + FIRST + SHARE * g + i - start]

        @pl.when(mine != g)
        def _():
            send(parts.at[g], found.at[mine], part_out, part_in, across(jnp.int32(g)))

    def step(p, carry):
        score_pair(p, taps_ref, gains, peak, total, series)
        for g in range(GROUP):
            due = SHARE * g + SHARE - 1
            if due < 2 * STEPS - 2:
                pl.when(p == due // 2)(functools.partial(pass_on, g))
        return carry

    lax.fori_loop(0, STEPS, step, 0)
    for g in range(GROUP):
        if SHARE * g + SHARE - 1 >= 2 * STEPS - 2:
            pass_on(g)
    found[mine] = parts[mine]
    wait_bytes(found.at[pl.ds(0, GROUP - 1)], part_in)
    plane_best[z] = jnp.max(found[...], axis=0)
    for i in range(1, LINE):
        send(plane_best.at[z], plane_best.at[z], line_out, line_in, along(i))
    finish_templates(peak, total, peak_ref, mean_ref)
    wait_bytes(plane_best.at[pl.ds(0, LINE - 1)], line_in)
    best[...] = jnp.max(plane_best[...], axis=0)
    for i in range(1, PLANE):
        to = (z * PLANE + lax.rem(xy + i, PLANE), tm)
        send(best, heard.at[xy], best_out, best_in, to)
    heard[xy] = best[...]
    wait_bytes(strain.at[pl.ds(0, LINE - 1)], lines_out)
    wait_bytes(strain.at[pl.ds(0, (GROUP - 1) * LINE)], plane_out)
    wait_bytes(parts.at[pl.ds(0, GROUP - 1)], part_out)
    wait_bytes(plane_best.at[pl.ds(0, LINE - 1)], line_out)
    wait_bytes(heard.at[pl.ds(0, PLANE - 1)], best_in)
    wait_bytes(heard.at[pl.ds(0, PLANE - 1)], best_out)
    silent = jnp.zeros((DET, LANES), jnp.float32)

    def block_of(i):
        inside = 0 <= i < PLANE * SHARE
        return heard[i // SHARE, i % SHARE, 0:DET, :] if inside else silent

    for c in range(SEG_CHUNKS):
        loud_ref[:, LANES * c : LANES * (c + 1)] = jnp.where(
            tm == 0, block_of(c - FIRST), block_of(c)
        )


def scratch(taps, templates):
    groups = templates // 8
    return [
        pltpu.VMEM((DET, CHUNKS, LANES), jnp.float32),
        pltpu.VMEM((DET, REL + 4, 8, LANES), jnp.float32),
        pltpu.VMEM((DET, taps, REL * LANES), jnp.bfloat16),
        pltpu.VMEM((groups, 16, taps), jnp.bfloat16),
        pltpu.VMEM((DET, groups, 8, LANES), jnp.float32),
        pltpu.VMEM((DET, groups, 8, LANES), jnp.float32),
        pltpu.VMEM((CHUNKS, SLOT, LANES), jnp.float32),
    ]


VMEM = pl.BlockSpec(memory_space=pltpu.VMEM)
SMEM = pl.BlockSpec(memory_space=pltpu.SMEM)
VMEM_LIMIT = 60 * 1024 * 1024


def per_device(
    raw_strain, psd_scale, basis_filters, recon_matrix, bin_taps, bin_band, bin_window, window_start
):
    n_bank, n_tm = lax.axis_size("bank"), lax.axis_size("tm")
    taps, templates = basis_filters.shape[1], recon_matrix.shape[3]
    stats = jax.ShapeDtypeStruct((DET, templates), jnp.float32)
    scalars = (bin_taps, bin_band, bin_window, window_start)
    if raw_strain.shape[2] == LANES and n_bank == SEG_CHUNKS and n_tm == 2:
        slots = pltpu.VMEM((CHUNKS, SLOT, LANES), jnp.float32)
        share = (SHARE, SLOT, LANES)
        return pl.pallas_call(
            linked_kernel,
            out_shape=(stats, stats, jax.ShapeDtypeStruct((DET, n_bank * LANES), jnp.float32)),
            in_specs=[pl.BlockSpec(memory_space=pltpu.HBM)] * 8,
            out_specs=(VMEM,) * 3,
            scratch_shapes=[pltpu.SMEM(v.shape, jnp.int32) for v in scalars]
            + [pltpu.SMEM((DET,), jnp.float32)]
            + [pltpu.VMEM(v.shape, v.dtype) for v in (raw_strain, basis_filters, recon_matrix)]
            + [slots, slots]
            + scratch(taps, templates)
            + [
                pltpu.VMEM((GROUP,) + share, jnp.float32),
                pltpu.VMEM((GROUP,) + share, jnp.float32),
                pltpu.VMEM((LINE,) + share, jnp.float32),
                pltpu.VMEM(share, jnp.float32),
                pltpu.VMEM((PLANE,) + share, jnp.float32),
                pltpu.SemaphoreType.DMA((8,)),
            ]
            + [pltpu.SemaphoreType.DMA] * 10,
            compiler_params=pltpu.CompilerParams(
                collective_id=0, has_side_effects=True, vmem_limit_bytes=VMEM_LIMIT
            ),
        )(*scalars, psd_scale.reshape(DET), raw_strain, basis_filters, recon_matrix)

    scaled = raw_strain * psd_scale
    whole = lax.all_gather(scaled, "bank", axis=2, tiled=True)
    whole = lax.all_gather(whole, "tm", axis=1, tiled=True)
    blocks = whole.reshape(DET, CHUNKS, LANES).transpose(1, 0, 2)
    blocks = jnp.pad(blocks, ((0, 0), (0, SLOT - DET), (0, 0)))
    peak, mean, loud = pl.pallas_call(
        local_kernel,
        out_shape=(stats, stats, jax.ShapeDtypeStruct((CHUNKS, SLOT, LANES), jnp.float32)),
        in_specs=[SMEM] * 4 + [VMEM] * 3,
        out_specs=(VMEM,) * 3,
        scratch_shapes=scratch(taps, templates),
        compiler_params=pltpu.CompilerParams(vmem_limit_bytes=VMEM_LIMIT),
    )(*scalars, blocks, basis_filters, recon_matrix)
    loud = lax.pmax(loud[:, :DET].transpose(1, 0, 2).reshape(DET, CHUNKS * LANES), ("bank", "tm"))
    length = CHUNKS * LANES // n_tm
    return peak, mean, lax.dynamic_slice_in_dim(loud, lax.axis_index("tm") * length, length, 1)


def solution(mesh):
    return jax.shard_map(
        per_device,
        mesh=mesh,
        in_specs=(
            P(None, "tm", "bank"),
            P(None, "tm", "bank"),
            P("bank", None, None),
            P("bank", None, None, "tm"),
            P("bank"),
            P("bank"),
            P("bank"),
            P(),
        ),
        out_specs=(P(None, ("bank", "tm")), P(None, ("bank", "tm")), P(None, "tm")),
        check_vma=False,
    )
```

```python
import functools

import jax
import jax.numpy as jnp
from jax import lax
from jax.experimental import pallas as pl
from jax.experimental.pallas import tpu as pltpu
from jax.sharding import PartitionSpec as P

EPSILON = 1e-06
LANES = 128
SEG_CHUNKS = 16
CHUNKS = 32
WIN = 2048
FIRST = 4
LAST = 28
STEPS = 9
REL = 2 * STEPS
PAD = 8
DET = 3
SLOT = 4
LINE, PLANE, GROUP = 4, 4, 8
SHARE = (LAST - FIRST) // GROUP
MESH = pl.DeviceIdType.MESH


def wait_bytes(ref, sem):
    pltpu.make_async_copy(ref, ref, sem).wait()


def fold_filters(basis_ref, recon_ref, taps, gains):
    features = basis_ref.shape[2]
    tap = lax.broadcasted_iota(jnp.int32, basis_ref.shape[1:], 0)
    basis = jnp.where(tap < taps, basis_ref[0].astype(jnp.float32), 0.0).astype(jnp.bfloat16)
    row = lax.broadcasted_iota(jnp.int32, (features, 2 * features), 0)
    col = lax.broadcasted_iota(jnp.int32, (features, 2 * features), 1)
    pairs = recon_ref[0].reshape(2 * features, recon_ref.shape[3])
    for c in range(2):
        spread = jnp.where(col == 2 * row + c, 1.0, 0.0).astype(jnp.bfloat16)
        wide = jnp.dot(basis, spread, preferred_element_type=jnp.float32).astype(jnp.bfloat16)
        g = jnp.dot(wide, pairs, preferred_element_type=jnp.float32)
        gt = g.T.astype(jnp.bfloat16)
        gains[:, 8 * c : 8 * c + 8, :] = gt.reshape(-1, 8, gt.shape[1])


def whiten_and_smooth(strain, d, rate, smooth):
    x = strain[:, d, :]
    ss = jnp.sum(jnp.sum(x * x, axis=0, keepdims=True), axis=1, keepdims=True)
    norm = jnp.sqrt(ss / (CHUNKS * LANES) + EPSILON)
    w = (x / norm).astype(jnp.bfloat16).astype(jnp.float32)
    lane = lax.broadcasted_iota(jnp.int32, w.shape, 1)
    row = lax.broadcasted_iota(jnp.int32, w.shape, 0)
    before = jnp.where(row == 0, 0.0, pltpu.roll(w, 1, 0))
    total = w
    for j in range(1, 4):
        late = jnp.where(lane < j, pltpu.roll(before, j, 1), pltpu.roll(w, j, 1))
        total = total + jnp.where(j < rate, late, 0.0)
    mean = total / rate.astype(jnp.float32)
    smooth[d] = mean.astype(jnp.bfloat16).astype(jnp.float32)


def lay_delays(d, rate, start, smooth, octet):
    count = REL + 4
    y = jnp.broadcast_to(smooth[d, pl.ds(start - 4, count), :][:, None, :], (count, 8, LANES))
    lane = lax.broadcasted_iota(jnp.int32, y.shape, 2)
    sub = lax.broadcasted_iota(jnp.int32, y.shape, 1)
    for bit in (1, 2, 4):
        shift = rate * bit
        r = pltpu.roll(y, shift, 2)
        late = jnp.where(lane < shift, jnp.concatenate([r[:1], r[:-1]], axis=0), r)
        y = jnp.where((sub & bit) != 0, late, y)
    octet[d] = y


def lay_taps(h, d, rate, offset, octet, taps_ref):
    lane = lax.broadcasted_iota(jnp.int32, (REL, 8, LANES), 2)
    when = lax.broadcasted_iota(jnp.int32, (REL, 8, LANES), 0) * LANES + lane
    inside = (when >= offset) & (when < offset + WIN)
    halves = []
    for e in range(2):
        eights = rate * (2 * h + e)
        back = eights // 16
        shift = 8 * (eights - 16 * back)
        r = pltpu.roll(octet[d, pl.ds(3 - back, REL + 1)], shift, 2)
        halves.append(jnp.where(inside, jnp.where(lane < shift, r[:-1], r[1:]), 0.0))
    both = jnp.concatenate(halves, axis=1).astype(jnp.bfloat16)
    at = pl.ds(pl.multiple_of(16 * h, 16), 16)
    for i in range(REL):
        taps_ref[d, at, LANES * i : LANES * (i + 1)] = both[i]


def score_pair(p, taps_ref, gains, peak, total, series):
    weights = gains[...]
    weights = weights.reshape(-1, weights.shape[2])
    for d in range(DET):
        at = pl.ds(pl.multiple_of(2 * LANES * p, 2 * LANES), 2 * LANES)
        snr = jnp.dot(weights, taps_ref[d, :, at], preferred_element_type=jnp.float32)
        snr = snr.reshape(-1, 2, 8, 2 * LANES)
        re, im = snr[:, 0], snr[:, 1]
        power = re * re + im * im
        left, right = power[:, :, :LANES], power[:, :, LANES:]
        peak[d] = jnp.maximum(peak[d], jnp.maximum(left, right))
        total[d] = total[d] + (left + right)
        loud = jnp.max(jnp.max(power, axis=0), axis=0, keepdims=True)
        series[PAD + 2 * p, d : d + 1, :] = loud[:, :LANES]
        series[PAD + 2 * p + 1, d : d + 1, :] = loud[:, LANES:]


def finish_templates(peak, total, peak_ref, mean_ref):
    for d in range(DET):
        top = peak[d].reshape(-1, LANES).T
        peak_ref[d : d + 1, :] = jnp.max(top, axis=0, keepdims=True)
        add = total[d].reshape(-1, LANES).T
        mean_ref[d : d + 1, :] = jnp.sum(add, axis=0, keepdims=True) * (1.0 / WIN)


def settings(taps_s, band_s, window_s, start_s):
    band = band_s[0]
    rate = jnp.where(band == 0, 1, jnp.where(band == 1, 2, 4)).astype(jnp.int32)
    opening = jnp.clip(start_s[window_s[0]], FIRST * LANES, LAST * LANES - WIN)
    start = opening // LANES
    return taps_s[0], rate, start, opening - LANES * start


def clear(peak, total, series):
    peak[...] = jnp.zeros_like(peak)
    total[...] = jnp.zeros_like(total)
    series[...] = jnp.zeros_like(series)


def lay_all(strain, rate, start, offset, smooth, octet, taps_ref):
    for d in range(DET):
        whiten_and_smooth(strain, d, rate, smooth)
    for d in range(DET):
        lay_delays(d, rate, start, smooth, octet)

    def body(h, carry):
        for d in range(DET):
            lay_taps(h, d, rate, offset, octet, taps_ref)
        return carry

    lax.fori_loop(0, 8, body, 0)


def local_kernel(
    taps_s, band_s, window_s, start_s, strain, basis_ref, recon_ref,
    peak_ref, mean_ref, loud_ref,
    smooth, octet, taps_ref, gains, peak, total, series,
):
    taps, rate, start, offset = settings(taps_s, band_s, window_s, start_s)
    clear(peak, total, series)
    fold_filters(basis_ref, recon_ref, taps, gains)
    lay_all(strain, rate, start, offset, smooth, octet, taps_ref)
    lax.fori_loop(
        0, STEPS, lambda p, c: (score_pair(p, taps_ref, gains, peak, total, series), c)[1], 0
    )
    loud_ref[...] = jnp.zeros_like(loud_ref)
    for q in range(FIRST, LAST):
        loud_ref[q] = series[PAD + q - start]
    finish_templates(peak, total, peak_ref, mean_ref)


def linked_kernel(
    taps_h, band_h, window_h, start_h, scale_h, raw_h, basis_h, recon_h,
    peak_ref, mean_ref, loud_ref,
    taps_s, band_s, window_s, start_s, scale_s, raw_ref, basis_ref, recon_ref,
    strain, ordered, smooth, octet, taps_ref, gains, peak, total, series,
    parts, found, best, heard,
    fetched, lines_out, lines_in, plane_out, plane_in,
    part_out, part_in, best_out, best_in,
):
    bank, tm = lax.axis_index("bank"), lax.axis_index("tm")
    z, xy = bank // PLANE, lax.rem(bank, PLANE)
    mine = tm * PLANE + xy

    def along(i):
        return (lax.rem(z + i, LINE) * PLANE + xy, tm)

    def across(g):
        return (z * PLANE + lax.rem(g, PLANE), g // PLANE)

    def send(src, dst, out, into, to):
        pltpu.make_async_remote_copy(
            src_ref=src, dst_ref=dst, send_sem=out, recv_sem=into,
            device_id=to, device_id_type=MESH,
        ).start()

    barrier = pltpu.get_barrier_semaphore()
    for i in range(1, LINE * PLANE):
        to = (lax.rem(bank + i, LINE * PLANE), tm)
        pl.semaphore_signal(barrier, inc=1, device_id=to, device_id_type=MESH)
    for i in range(PLANE):
        to = (z * PLANE + lax.rem(xy + i, PLANE), 1 - tm)
        pl.semaphore_signal(barrier, inc=1, device_id=to, device_id_type=MESH)
    pairs = (
        (scale_h, scale_s), (raw_h, raw_ref), (taps_h, taps_s), (band_h, band_s),
        (window_h, window_s), (start_h, start_s), (basis_h, basis_ref), (recon_h, recon_ref),
    )
    fetches = [pltpu.make_async_copy(a, b, fetched.at[i]) for i, (a, b) in enumerate(pairs)]
    for fetch in fetches:
        fetch.start()
    fetches[0].wait()
    fetches[1].wait()
    block = jnp.concatenate([raw_ref[d] * scale_s[d] for d in range(DET)], axis=0)
    here = mine * LINE + z
    strain[here] = jnp.concatenate([block, jnp.zeros((SLOT - DET, LANES), jnp.float32)], axis=0)
    pl.semaphore_wait(barrier, LINE * PLANE - 1 + PLANE)
    for i in range(1, LINE):
        send(strain.at[here], strain.at[here], lines_out, lines_in, along(i))
    clear(peak, total, series)
    for fetch in fetches[2:]:
        fetch.wait()
    taps, rate, start, offset = settings(taps_s, band_s, window_s, start_s)
    run = strain.at[pl.ds(mine * LINE, LINE)]
    wait_bytes(strain.at[pl.ds(0, LINE - 1)], lines_in)
    for i in range(1, GROUP):
        send(run, run, plane_out, plane_in, across(lax.rem(mine + i, GROUP)))
    fold_filters(basis_ref, recon_ref, taps, gains)
    wait_bytes(strain.at[pl.ds(0, (GROUP - 1) * LINE)], plane_in)
    for q in range(CHUNKS):
        t, line, spot = q // SEG_CHUNKS, q % SEG_CHUNKS // PLANE, q % PLANE
        ordered[q] = strain[(t * PLANE + spot) * LINE + line]
    lay_all(ordered, rate, start, offset, smooth, octet, taps_ref)

    def pass_on(g):
        for i in range(SHARE):
            parts[g, i] = series[PAD + FIRST + SHARE * g + i - start]

        @pl.when(mine != g)
        def _():
            send(parts.at[g], found.at[mine], part_out, part_in, across(jnp.int32(g)))

    def step(p, carry):
        score_pair(p, taps_ref, gains, peak, total, series)
        for g in range(GROUP):
            due = SHARE * g + SHARE - 1
            if due < 2 * STEPS - 2:
                pl.when(p == due // 2)(functools.partial(pass_on, g))
        return carry

    lax.fori_loop(0, STEPS, step, 0)
    for g in range(GROUP):
        if SHARE * g + SHARE - 1 >= 2 * STEPS - 2:
            pass_on(g)
    found[mine] = parts[mine]
    wait_bytes(found.at[pl.ds(0, GROUP - 1)], part_in)
    best[...] = jnp.max(found[...], axis=0)
    for i in range(1, LINE * PLANE):
        to = (lax.rem(bank + i, LINE * PLANE), tm)
        send(best, heard.at[bank], best_out, best_in, to)
    heard[bank] = best[...]
    finish_templates(peak, total, peak_ref, mean_ref)
    wait_bytes(strain.at[pl.ds(0, LINE - 1)], lines_out)
    wait_bytes(strain.at[pl.ds(0, (GROUP - 1) * LINE)], plane_out)
    wait_bytes(parts.at[pl.ds(0, GROUP - 1)], part_out)
    wait_bytes(heard.at[pl.ds(0, LINE * PLANE - 1)], best_in)
    wait_bytes(heard.at[pl.ds(0, LINE * PLANE - 1)], best_out)
    silent = jnp.zeros((DET, LANES), jnp.float32)

    def block_of(i):
        inside = 0 <= i < PLANE * SHARE
        if not inside:
            return silent
        planes = [heard[PLANE * k + i // SHARE, i % SHARE, 0:DET, :] for k in range(LINE)]
        return functools.reduce(jnp.maximum, planes)

    for c in range(SEG_CHUNKS):
        loud_ref[:, LANES * c : LANES * (c + 1)] = jnp.where(
            tm == 0, block_of(c - FIRST), block_of(c)
        )


def scratch(taps, templates):
    groups = templates // 8
    return [
        pltpu.VMEM((DET, CHUNKS, LANES), jnp.float32),
        pltpu.VMEM((DET, REL + 4, 8, LANES), jnp.float32),
        pltpu.VMEM((DET, taps, REL * LANES), jnp.bfloat16),
        pltpu.VMEM((groups, 16, taps), jnp.bfloat16),
        pltpu.VMEM((DET, groups, 8, LANES), jnp.float32),
        pltpu.VMEM((DET, groups, 8, LANES), jnp.float32),
        pltpu.VMEM((CHUNKS, SLOT, LANES), jnp.float32),
    ]


VMEM = pl.BlockSpec(memory_space=pltpu.VMEM)
SMEM = pl.BlockSpec(memory_space=pltpu.SMEM)
VMEM_LIMIT = 60 * 1024 * 1024


def per_device(
    raw_strain, psd_scale, basis_filters, recon_matrix, bin_taps, bin_band, bin_window, window_start
):
    n_bank, n_tm = lax.axis_size("bank"), lax.axis_size("tm")
    taps, templates = basis_filters.shape[1], recon_matrix.shape[3]
    stats = jax.ShapeDtypeStruct((DET, templates), jnp.float32)
    scalars = (bin_taps, bin_band, bin_window, window_start)
    if raw_strain.shape[2] == LANES and n_bank == SEG_CHUNKS and n_tm == 2:
        slots = pltpu.VMEM((CHUNKS, SLOT, LANES), jnp.float32)
        share = (SHARE, SLOT, LANES)
        return pl.pallas_call(
            linked_kernel,
            out_shape=(
                pltpu.VMEM(stats.shape, jnp.float32),
                pltpu.VMEM(stats.shape, jnp.float32),
                pltpu.VMEM((DET, n_bank * LANES), jnp.float32),
            ),
            in_specs=[pl.BlockSpec(memory_space=pltpu.HBM)] * 8,
            out_specs=(VMEM,) * 3,
            scratch_shapes=[pltpu.SMEM(v.shape, jnp.int32) for v in scalars]
            + [pltpu.SMEM((DET,), jnp.float32)]
            + [pltpu.VMEM(v.shape, v.dtype) for v in (raw_strain, basis_filters, recon_matrix)]
            + [slots, slots]
            + scratch(taps, templates)
            + [
                pltpu.VMEM((GROUP,) + share, jnp.float32),
                pltpu.VMEM((GROUP,) + share, jnp.float32),
                pltpu.VMEM(share, jnp.float32),
                pltpu.VMEM((LINE * PLANE,) + share, jnp.float32),
                pltpu.SemaphoreType.DMA((8,)),
            ]
            + [pltpu.SemaphoreType.DMA] * 8,
            compiler_params=pltpu.CompilerParams(
                collective_id=0, has_side_effects=True, vmem_limit_bytes=VMEM_LIMIT
            ),
        )(*scalars, psd_scale.reshape(DET), raw_strain, basis_filters, recon_matrix)

    scaled = raw_strain * psd_scale
    whole = lax.all_gather(scaled, "bank", axis=2, tiled=True)
    whole = lax.all_gather(whole, "tm", axis=1, tiled=True)
    blocks = whole.reshape(DET, CHUNKS, LANES).transpose(1, 0, 2)
    blocks = jnp.pad(blocks, ((0, 0), (0, SLOT - DET), (0, 0)))
    peak, mean, loud = pl.pallas_call(
        local_kernel,
        out_shape=(stats, stats, jax.ShapeDtypeStruct((CHUNKS, SLOT, LANES), jnp.float32)),
        in_specs=[SMEM] * 4 + [VMEM] * 3,
        out_specs=(VMEM,) * 3,
        scratch_shapes=scratch(taps, templates),
        compiler_params=pltpu.CompilerParams(vmem_limit_bytes=VMEM_LIMIT),
    )(*scalars, blocks, basis_filters, recon_matrix)
    loud = lax.pmax(loud[:, :DET].transpose(1, 0, 2).reshape(DET, CHUNKS * LANES), ("bank", "tm"))
    length = CHUNKS * LANES // n_tm
    return peak, mean, lax.dynamic_slice_in_dim(loud, lax.axis_index("tm") * length, length, 1)


def solution(mesh):
    return jax.shard_map(
        per_device,
        mesh=mesh,
        in_specs=(
            P(None, "tm", "bank"),
            P(None, "tm", "bank"),
            P("bank", None, None),
            P("bank", None, None, "tm"),
            P("bank"),
            P("bank"),
            P("bank"),
            P(),
        ),
        out_specs=(P(None, ("bank", "tm")), P(None, ("bank", "tm")), P(None, "tm")),
        check_vma=False,
    )
```

```python
import functools

import jax
import jax.numpy as jnp
from jax import lax
from jax.experimental import pallas as pl
from jax.experimental.pallas import tpu as pltpu
from jax.sharding import PartitionSpec as P

EPSILON = 1e-06
LANES = 128
SEG_CHUNKS = 16
CHUNKS = 32
WIN = 2048
FIRST = 4
LAST = 28
STEPS = 9
REL = 2 * STEPS
PAD = 8
DET = 3
SLOT = 4
LINE, PLANE, GROUP = 4, 4, 8
SHARE = (LAST - FIRST) // GROUP
MESH = pl.DeviceIdType.MESH


def wait_bytes(ref, sem):
    pltpu.make_async_copy(ref, ref, sem).wait()


def fold_filters(basis_ref, recon_ref, taps, gains):
    features = basis_ref.shape[2]
    tap = lax.broadcasted_iota(jnp.int32, basis_ref.shape[1:], 0)
    basis = jnp.where(tap < taps, basis_ref[0].astype(jnp.float32), 0.0).astype(jnp.bfloat16)
    row = lax.broadcasted_iota(jnp.int32, (features, 2 * features), 0)
    col = lax.broadcasted_iota(jnp.int32, (features, 2 * features), 1)
    pairs = recon_ref[0].reshape(2 * features, recon_ref.shape[3])
    for c in range(2):
        spread = jnp.where(col == 2 * row + c, 1.0, 0.0).astype(jnp.bfloat16)
        wide = jnp.dot(basis, spread, preferred_element_type=jnp.float32).astype(jnp.bfloat16)
        g = jnp.dot(wide, pairs, preferred_element_type=jnp.float32)
        gt = g.T.astype(jnp.bfloat16)
        gains[:, 8 * c : 8 * c + 8, :] = gt.reshape(-1, 8, gt.shape[1])


def whiten_and_smooth(strain, d, rate, smooth):
    x = strain[:, d, :]
    ss = jnp.sum(jnp.sum(x * x, axis=0, keepdims=True), axis=1, keepdims=True)
    norm = jnp.sqrt(ss / (CHUNKS * LANES) + EPSILON)
    w = (x / norm).astype(jnp.bfloat16).astype(jnp.float32)
    lane = lax.broadcasted_iota(jnp.int32, w.shape, 1)
    row = lax.broadcasted_iota(jnp.int32, w.shape, 0)
    before = jnp.where(row == 0, 0.0, pltpu.roll(w, 1, 0))
    total = w
    for j in range(1, 4):
        late = jnp.where(lane < j, pltpu.roll(before, j, 1), pltpu.roll(w, j, 1))
        total = total + jnp.where(j < rate, late, 0.0)
    mean = total / rate.astype(jnp.float32)
    smooth[d] = mean.astype(jnp.bfloat16).astype(jnp.float32)


def lay_delays(d, rate, start, smooth, octet):
    count = REL + 4
    y = jnp.broadcast_to(smooth[d, pl.ds(start - 4, count), :][:, None, :], (count, 8, LANES))
    lane = lax.broadcasted_iota(jnp.int32, y.shape, 2)
    sub = lax.broadcasted_iota(jnp.int32, y.shape, 1)
    for bit in (1, 2, 4):
        shift = rate * bit
        r = pltpu.roll(y, shift, 2)
        late = jnp.where(lane < shift, jnp.concatenate([r[:1], r[:-1]], axis=0), r)
        y = jnp.where((sub & bit) != 0, late, y)
    octet[d] = y


def lay_taps(h, d, rate, offset, octet, taps_ref):
    lane = lax.broadcasted_iota(jnp.int32, (REL, 8, LANES), 2)
    when = lax.broadcasted_iota(jnp.int32, (REL, 8, LANES), 0) * LANES + lane
    inside = (when >= offset) & (when < offset + WIN)
    halves = []
    for e in range(2):
        eights = rate * (2 * h + e)
        back = eights // 16
        shift = 8 * (eights - 16 * back)
        r = pltpu.roll(octet[d, pl.ds(3 - back, REL + 1)], shift, 2)
        halves.append(jnp.where(inside, jnp.where(lane < shift, r[:-1], r[1:]), 0.0))
    both = jnp.concatenate(halves, axis=1).astype(jnp.bfloat16)
    at = pl.ds(pl.multiple_of(16 * h, 16), 16)
    for i in range(REL):
        taps_ref[d, at, LANES * i : LANES * (i + 1)] = both[i]


def score_pair(p, taps_ref, gains, peak, total, series):
    weights = gains[...]
    weights = weights.reshape(-1, weights.shape[2])
    for d in range(DET):
        at = pl.ds(pl.multiple_of(2 * LANES * p, 2 * LANES), 2 * LANES)
        snr = jnp.dot(weights, taps_ref[d, :, at], preferred_element_type=jnp.float32)
        snr = snr.reshape(-1, 2, 8, 2 * LANES)
        re, im = snr[:, 0], snr[:, 1]
        power = re * re + im * im
        left, right = power[:, :, :LANES], power[:, :, LANES:]
        peak[d] = jnp.maximum(peak[d], jnp.maximum(left, right))
        total[d] = total[d] + (left + right)
        loud = jnp.max(jnp.max(power, axis=0), axis=0, keepdims=True)
        series[PAD + 2 * p, d : d + 1, :] = loud[:, :LANES]
        series[PAD + 2 * p + 1, d : d + 1, :] = loud[:, LANES:]


def finish_templates(peak, total, peak_ref, mean_ref):
    for d in range(DET):
        top = peak[d].reshape(-1, LANES).T
        peak_ref[d : d + 1, :] = jnp.max(top, axis=0, keepdims=True)
        add = total[d].reshape(-1, LANES).T
        mean_ref[d : d + 1, :] = jnp.sum(add, axis=0, keepdims=True) * (1.0 / WIN)


def settings(taps_s, band_s, window_s, start_s):
    band = band_s[0]
    rate = jnp.where(band == 0, 1, jnp.where(band == 1, 2, 4)).astype(jnp.int32)
    opening = jnp.clip(start_s[window_s[0]], FIRST * LANES, LAST * LANES - WIN)
    start = opening // LANES
    return taps_s[0], rate, start, opening - LANES * start


def clear(peak, total, series):
    peak[...] = jnp.zeros_like(peak)
    total[...] = jnp.zeros_like(total)
    series[...] = jnp.zeros_like(series)


def lay_all(strain, rate, start, offset, smooth, octet, taps_ref):
    for d in range(DET):
        whiten_and_smooth(strain, d, rate, smooth)
    for d in range(DET):
        lay_delays(d, rate, start, smooth, octet)

    def body(h, carry):
        for d in range(DET):
            lay_taps(h, d, rate, offset, octet, taps_ref)
        return carry

    lax.fori_loop(0, 8, body, 0)


def local_kernel(
    taps_s, band_s, window_s, start_s, strain, basis_ref, recon_ref,
    peak_ref, mean_ref, loud_ref,
    smooth, octet, taps_ref, gains, peak, total, series,
):
    taps, rate, start, offset = settings(taps_s, band_s, window_s, start_s)
    clear(peak, total, series)
    fold_filters(basis_ref, recon_ref, taps, gains)
    lay_all(strain, rate, start, offset, smooth, octet, taps_ref)
    lax.fori_loop(
        0, STEPS, lambda p, c: (score_pair(p, taps_ref, gains, peak, total, series), c)[1], 0
    )
    loud_ref[...] = jnp.zeros_like(loud_ref)
    for q in range(FIRST, LAST):
        loud_ref[q] = series[PAD + q - start]
    finish_templates(peak, total, peak_ref, mean_ref)


def linked_kernel(
    taps_h, band_h, window_h, start_h, scale_h, raw_h, basis_h, recon_h,
    peak_ref, mean_ref, loud_ref,
    taps_s, band_s, window_s, start_s, scale_s, raw_ref, basis_ref, recon_ref,
    strain, ordered, smooth, octet, taps_ref, gains, peak, total, series,
    parts, found, best, heard,
    fetched, lines_out, lines_in, plane_out, plane_in,
    part_out, part_in, best_out, best_in,
):
    bank, tm = lax.axis_index("bank"), lax.axis_index("tm")
    z, xy = bank // PLANE, lax.rem(bank, PLANE)
    mine = tm * PLANE + xy

    def along(i):
        return (lax.rem(z + i, LINE) * PLANE + xy, tm)

    def across(g):
        return (z * PLANE + lax.rem(g, PLANE), g // PLANE)

    def send(src, dst, out, into, to):
        pltpu.make_async_remote_copy(
            src_ref=src, dst_ref=dst, send_sem=out, recv_sem=into,
            device_id=to, device_id_type=MESH,
        ).start()

    barrier = pltpu.get_barrier_semaphore()
    for i in range(1, LINE * PLANE):
        to = (lax.rem(bank + i, LINE * PLANE), tm)
        pl.semaphore_signal(barrier, inc=1, device_id=to, device_id_type=MESH)
    for i in range(PLANE):
        to = (z * PLANE + lax.rem(xy + i, PLANE), 1 - tm)
        pl.semaphore_signal(barrier, inc=1, device_id=to, device_id_type=MESH)
    pairs = (
        (scale_h, scale_s), (raw_h, raw_ref), (taps_h, taps_s), (band_h, band_s),
        (window_h, window_s), (start_h, start_s), (basis_h, basis_ref), (recon_h, recon_ref),
    )
    fetches = [pltpu.make_async_copy(a, b, fetched.at[i]) for i, (a, b) in enumerate(pairs)]
    for fetch in fetches:
        fetch.start()
    fetches[0].wait()
    fetches[1].wait()
    block = jnp.concatenate([raw_ref[d] * scale_s[d] for d in range(DET)], axis=0)
    here = mine * LINE + z
    strain[here] = jnp.concatenate([block, jnp.zeros((SLOT - DET, LANES), jnp.float32)], axis=0)
    pl.semaphore_wait(barrier, LINE * PLANE - 1 + PLANE)
    for i in range(1, LINE):
        send(strain.at[here], strain.at[here], lines_out, lines_in, along(i))
    clear(peak, total, series)
    for fetch in fetches[2:]:
        fetch.wait()
    taps, rate, start, offset = settings(taps_s, band_s, window_s, start_s)
    run = strain.at[pl.ds(mine * LINE, LINE)]
    wait_bytes(strain.at[pl.ds(0, LINE - 1)], lines_in)
    for i in range(1, GROUP):
        send(run, run, plane_out, plane_in, across(lax.rem(mine + i, GROUP)))
    fold_filters(basis_ref, recon_ref, taps, gains)
    wait_bytes(strain.at[pl.ds(0, (GROUP - 1) * LINE)], plane_in)
    for q in range(CHUNKS):
        t, line, spot = q // SEG_CHUNKS, q % SEG_CHUNKS // PLANE, q % PLANE
        ordered[q] = strain[(t * PLANE + spot) * LINE + line]
    lay_all(ordered, rate, start, offset, smooth, octet, taps_ref)

    def pass_on(g):
        rows = [series[PAD + FIRST + SHARE * g + i - start] for i in range(SHARE)]
        rows.append(jnp.zeros((SLOT, LANES), jnp.float32))
        parts[g] = jnp.concatenate(rows, axis=0).astype(jnp.bfloat16)

        @pl.when(mine != g)
        def _():
            send(parts.at[g], found.at[mine], part_out, part_in, across(jnp.int32(g)))

    def step(p, carry):
        score_pair(p, taps_ref, gains, peak, total, series)
        for g in range(GROUP):
            due = SHARE * g + SHARE - 1
            if due < 2 * STEPS - 2:
                pl.when(p == due // 2)(functools.partial(pass_on, g))
        return carry

    lax.fori_loop(0, STEPS, step, 0)
    for g in range(GROUP):
        if SHARE * g + SHARE - 1 >= 2 * STEPS - 2:
            pass_on(g)
    found[mine] = parts[mine]
    wait_bytes(found.at[pl.ds(0, GROUP - 1)], part_in)
    best[...] = jnp.max(found[...].astype(jnp.float32), axis=0).astype(jnp.bfloat16)
    for i in range(1, LINE * PLANE):
        to = (lax.rem(bank + i, LINE * PLANE), tm)
        send(best, heard.at[bank], best_out, best_in, to)
    heard[bank] = best[...]
    finish_templates(peak, total, peak_ref, mean_ref)
    wait_bytes(strain.at[pl.ds(0, LINE - 1)], lines_out)
    wait_bytes(strain.at[pl.ds(0, (GROUP - 1) * LINE)], plane_out)
    wait_bytes(parts.at[pl.ds(0, GROUP - 1)], part_out)
    wait_bytes(heard.at[pl.ds(0, LINE * PLANE - 1)], best_in)
    wait_bytes(heard.at[pl.ds(0, LINE * PLANE - 1)], best_out)
    silent = jnp.zeros((DET, LANES), jnp.float32)

    merged = [
        functools.reduce(
            jnp.maximum, [heard[PLANE * k + j].astype(jnp.float32) for k in range(LINE)]
        )
        for j in range(PLANE)
    ]

    def block_of(i):
        inside = 0 <= i < PLANE * SHARE
        if not inside:
            return silent
        at = SLOT * (i % SHARE)
        return merged[i // SHARE][at : at + DET, :]

    for c in range(SEG_CHUNKS):
        loud_ref[:, LANES * c : LANES * (c + 1)] = jnp.where(
            tm == 0, block_of(c - FIRST), block_of(c)
        )


def scratch(taps, templates):
    groups = templates // 8
    return [
        pltpu.VMEM((DET, CHUNKS, LANES), jnp.float32),
        pltpu.VMEM((DET, REL + 4, 8, LANES), jnp.float32),
        pltpu.VMEM((DET, taps, REL * LANES), jnp.bfloat16),
        pltpu.VMEM((groups, 16, taps), jnp.bfloat16),
        pltpu.VMEM((DET, groups, 8, LANES), jnp.float32),
        pltpu.VMEM((DET, groups, 8, LANES), jnp.float32),
        pltpu.VMEM((CHUNKS, SLOT, LANES), jnp.float32),
    ]


VMEM = pl.BlockSpec(memory_space=pltpu.VMEM)
SMEM = pl.BlockSpec(memory_space=pltpu.SMEM)
VMEM_LIMIT = 60 * 1024 * 1024


def per_device(
    raw_strain, psd_scale, basis_filters, recon_matrix, bin_taps, bin_band, bin_window, window_start
):
    n_bank, n_tm = lax.axis_size("bank"), lax.axis_size("tm")
    taps, templates = basis_filters.shape[1], recon_matrix.shape[3]
    stats = jax.ShapeDtypeStruct((DET, templates), jnp.float32)
    scalars = (bin_taps, bin_band, bin_window, window_start)
    if raw_strain.shape[2] == LANES and n_bank == SEG_CHUNKS and n_tm == 2:
        slots = pltpu.VMEM((CHUNKS, SLOT, LANES), jnp.float32)
        share = (SHARE * SLOT + SLOT, LANES)
        return pl.pallas_call(
            linked_kernel,
            out_shape=(
                pltpu.VMEM(stats.shape, jnp.float32),
                pltpu.VMEM(stats.shape, jnp.float32),
                pltpu.VMEM((DET, n_bank * LANES), jnp.float32),
            ),
            in_specs=[pl.BlockSpec(memory_space=pltpu.HBM)] * 8,
            out_specs=(VMEM,) * 3,
            scratch_shapes=[pltpu.SMEM(v.shape, jnp.int32) for v in scalars]
            + [pltpu.SMEM((DET,), jnp.float32)]
            + [pltpu.VMEM(v.shape, v.dtype) for v in (raw_strain, basis_filters, recon_matrix)]
            + [slots, slots]
            + scratch(taps, templates)
            + [
                pltpu.VMEM((GROUP,) + share, jnp.bfloat16),
                pltpu.VMEM((GROUP,) + share, jnp.bfloat16),
                pltpu.VMEM(share, jnp.bfloat16),
                pltpu.VMEM((LINE * PLANE,) + share, jnp.bfloat16),
                pltpu.SemaphoreType.DMA((8,)),
            ]
            + [pltpu.SemaphoreType.DMA] * 8,
            compiler_params=pltpu.CompilerParams(
                collective_id=0, has_side_effects=True, vmem_limit_bytes=VMEM_LIMIT
            ),
        )(*scalars, psd_scale.reshape(DET), raw_strain, basis_filters, recon_matrix)

    scaled = raw_strain * psd_scale
    whole = lax.all_gather(scaled, "bank", axis=2, tiled=True)
    whole = lax.all_gather(whole, "tm", axis=1, tiled=True)
    blocks = whole.reshape(DET, CHUNKS, LANES).transpose(1, 0, 2)
    blocks = jnp.pad(blocks, ((0, 0), (0, SLOT - DET), (0, 0)))
    peak, mean, loud = pl.pallas_call(
        local_kernel,
        out_shape=(stats, stats, jax.ShapeDtypeStruct((CHUNKS, SLOT, LANES), jnp.float32)),
        in_specs=[SMEM] * 4 + [VMEM] * 3,
        out_specs=(VMEM,) * 3,
        scratch_shapes=scratch(taps, templates),
        compiler_params=pltpu.CompilerParams(vmem_limit_bytes=VMEM_LIMIT),
    )(*scalars, blocks, basis_filters, recon_matrix)
    loud = lax.pmax(loud[:, :DET].transpose(1, 0, 2).reshape(DET, CHUNKS * LANES), ("bank", "tm"))
    length = CHUNKS * LANES // n_tm
    return peak, mean, lax.dynamic_slice_in_dim(loud, lax.axis_index("tm") * length, length, 1)


def solution(mesh):
    return jax.shard_map(
        per_device,
        mesh=mesh,
        in_specs=(
            P(None, "tm", "bank"),
            P(None, "tm", "bank"),
            P("bank", None, None),
            P("bank", None, None, "tm"),
            P("bank"),
            P("bank"),
            P("bank"),
            P(),
        ),
        out_specs=(P(None, ("bank", "tm")), P(None, ("bank", "tm")), P(None, "tm")),
        check_vma=False,
    )
```
